32 devices in a mesh: groups: 1, tp: 32 (over z, y, x, core).
Axes of the slice: x: 2, y: 2, z: 4, core: 2. Of those that a mesh axis runs over, the one named last changes fastest.
Arguments:
- hidden_in: bfloat16 [192, 3584], P(('groups', 'tp')), may hold values from -6 to 6
- norm_dense: float32 [3584], replicated, may hold values from 0.1 to 1.9
- dense_gate: bfloat16 [3584, 18432], P(None, 'tp'), may hold values from -0.09375 to 0.09375
- dense_up: bfloat16 [3584, 18432], P(None, 'tp'), may hold values from -0.09375 to 0.09375
- dense_down: bfloat16 [18432, 3584], P('tp'), may hold values from -0.046875 to 0.046875
- norm_moe: float32 [3584], replicated, may hold values from 0.1 to 1.9
- expert_gate: bfloat16 [32, 3584, 256], P('tp'), may hold values from -0.09375 to 0.09375
- expert_up: bfloat16 [32, 3584, 256], P('tp'), may hold values from -0.09375 to 0.09375
- expert_down: bfloat16 [32, 256, 3584], P('tp'), may hold values from -0.1875 to 0.1875
- expert_ids: int32 [192, 4], P(('groups', 'tp')), may hold values from 0 to 7, all different within a row; in each aligned block of 6 rows (0 to 5, 6 to 11, ...) at most 4 rows name the same one
- gate_weights: float32 [192, 4], P(('groups', 'tp')), may hold values from 0.1 to 1
- placement: int32 [32], replicated, may hold values from 0 to 31, each once
- request_counts: int32 [32], P('groups'), may hold values from 1 to 2, 42 in all
Outputs:
- layer_out: bfloat16 [192, 3584], P(('groups', 'tp'))
The draws below stay inside these ranges and needn't reach their ends.
Inputs may be any that keep to these rules, and one draw needn't show every extreme that they name: `expert_ids`: in each aligned block of 6 rows (the rows of one device), no expert is named by more than 4 rows; some expert reaches 4 in some block. The 4 experts of a row differ. `placement`: A permutation: each device holds exactly one expert slice. `request_counts`: the counts of each group (serving replica) sum to 42; the largest is exactly 2.
All inputs are finite; a program needn't handle non-finite values.
Results may differ from the reference program's by a relative error of at most 0.0071.
Values may be sent and summed in bfloat16 or wider, within the bound.
A program may use at most 64 MiB of HBM per device.

```python
import math
import jax
import jax.numpy as jnp
import numpy as np
from jax import lax

D = 3584
FF = 18432
FF_E = 1024
SPLIT = 4
TOP = 4
DRAFT = 3
REQ_DEV = 2
SLICE = 256
EXPERTS = 8
ROWS_DEV = 6
ROWS = 192
CAPACITY = 4
TOTAL_REQ = 42
N_TP = 32


def level_of(key, dims, cuts, smallest, top_value):
    def one(dim, blocks):
        steps = jax.random.uniform(jax.random.fold_in(jax.random.fold_in(key, 6), dim), (blocks,), jnp.float32, smallest / len(cuts), top_value / len(cuts))
        return jnp.repeat(jnp.exp(steps), dims[dim] // blocks).reshape((-1,) + (1,) * (len(dims) - dim - 1))

    factor_of = one(*cuts[0])
    for cut in cuts[1:]:
        factor_of = factor_of * one(*cut)
    return factor_of


def length_profile(count, total, bound, lean):
    portions = [(1 << 20) // math.isqrt(rank ** lean) + 1 for rank in range(2, count + 1)]
    rest, given = total - bound - (count - 1), [1] * (count - 1)
    while rest > 0:
        movable = [i for i in range(count - 1) if given[i] < bound]
        pool, left = sum([portions[i] for i in movable]), rest
        for i in movable:
            addition = min(bound - given[i], max(1, left * portions[i] // pool), rest)
            given[i] = given[i] + addition
            rest = rest - addition
    return np.array([bound] + given)


def uneven_parts(own_key, number_of, total, most, slope):
    if number_of == 2:
        one = jax.random.randint(own_key, (), max(1, total - most), min(most, total - 1) + 1)
        return jnp.stack([one, total - one])
    lengths = jnp.asarray(length_profile(number_of, total, most, slope), jnp.int32)
    pairs = (number_of - 1) // 2
    donor, receiver = lengths[1:1 + 2 * pairs:2], lengths[2:2 + 2 * pairs:2]
    margin = jnp.minimum(donor - 1, most - receiver)
    passed = jax.random.randint(jax.random.fold_in(own_key, 1), (pairs,), 0, 1 << 20) % (margin + 1)
    lengths = lengths.at[1:1 + 2 * pairs:2].set(donor - passed).at[2:2 + 2 * pairs:2].set(receiver + passed)
    return lengths[jax.random.permutation(jax.random.fold_in(own_key, 2), number_of)]


def assign_block(rng, own, number, rows, amount, top, limit, skew):
    sequence = jax.random.permutation(rng, amount)
    heavy_load, usual = load_shares(amount, rows * top, limit, skew, True), load_shares(amount, rows * top, limit, skew, False)
    places = jnp.arange(amount)

    def named(sizes, turn):
        used = int((sizes > 0).sum())
        fixed = max(1, used // 4)
        shifted = fixed + (places - fixed + turn * (used - fixed)) % max(1, amount - fixed)
        return jnp.zeros((amount,), jnp.int32).at[sequence[jnp.where(places < fixed, places, shifted)]].set(jnp.asarray(sizes, jnp.int32))

    sizes = jnp.where(number % 4 == 0, named(heavy_load, number // 4), named(usual, number - number // 4 - 1))
    mixed = jax.random.permutation(jax.random.fold_in(own, 3), amount)
    source_of, taker = mixed[0:amount // 2 * 2:2], mixed[1:amount // 2 * 2:2]
    slack = jnp.minimum(sizes[source_of] - 1, limit - sizes[taker]) // 2
    slack = jnp.where((source_of == sequence[0]) | (taker == sequence[0]) | (sizes[taker] == 0), 0, jnp.maximum(slack, 0))
    shifted = jax.random.randint(jax.random.fold_in(own, 4), (amount // 2,), 0, 1 << 20) % (slack + 1)
    sizes = sizes.at[source_of].add(-shifted).at[taker].add(shifted)
    items = jnp.searchsorted(jnp.cumsum(sizes), jnp.arange(rows * top), side="right").astype(jnp.int32)
    table = items.reshape(top, rows).T
    table = table[jax.random.permutation(jax.random.fold_in(own, 1), rows)]
    turn = jax.random.randint(jax.random.fold_in(own, 2), (rows, 1), 0, top)
    return jnp.take_along_axis(table, (jnp.arange(top)[None, :] + turn) % top, axis=1)


def load_shares(number_of, total, bound, lean, full):
    weights = [(1 << 20) // math.isqrt(standing ** lean) + 1 for standing in range(1, number_of + 1)]
    largest = bound if full else min(bound, max(-(-total // number_of), total * weights[0] // sum(weights)))
    least = 1 if total - largest >= number_of - 1 else 0
    counts, rest = [largest] + [least] * (number_of - 1), total - largest - least * (number_of - 1)
    while rest > 0:
        candidates = [i for i in range(1, number_of) if counts[i] < largest] or [i for i in range(1, number_of) if counts[i] < bound]
        whole, remaining = sum([weights[i] for i in candidates]), rest
        for i in candidates:
            more = min(bound - counts[i], max(1, remaining * weights[i] // whole), rest)
            counts[i] = counts[i] + more
            rest = rest - more
    return np.array(counts)


def gaussian(rng, dims, scale, most, split=(), kind=jnp.bfloat16):
    entries = jax.random.normal(rng, dims, jnp.float32) * scale
    if len(split) > 0:
        entries = level_of(rng, dims, split, -0.22, 0.18) * entries
    return jnp.clip(entries, min=-most, max=most).astype(kind)


def setup_inputs(seed: int = 0, part: int = 0) -> dict:
    key_of = jax.random.split(jax.random.key(seed), 14)
    part_keys = jax.random.split(jax.random.fold_in(key_of[13], part), 14)
    hidden_in = gaussian(part_keys[0], (ROWS, D), 1.0, 6.0, ((0, 32),))
    norm_dense = jnp.clip(1.0 + 0.18 * jax.random.normal(key_of[1], (D,), jnp.float32), 0.1, 1.9)
    dense_gate = gaussian(key_of[2], (D, FF), D ** -0.5, 0.09375, ((1, 32),))
    dense_up = gaussian(key_of[3], (D, FF), D ** -0.5, 0.09375, ((1, 32),))
    dense_down = gaussian(key_of[4], (FF, D), FF ** -0.5, 0.046875, ((0, 32),))
    norm_moe = jnp.clip(1.0 + 0.18 * jax.random.normal(key_of[5], (D,), jnp.float32), 0.1, 1.9)
    expert_gate = gaussian(key_of[6], (N_TP, D, SLICE), D ** -0.5, 0.09375, ((0, 32),))
    expert_up = gaussian(key_of[7], (N_TP, D, SLICE), D ** -0.5, 0.09375, ((0, 32),))
    expert_down = gaussian(key_of[8], (N_TP, SLICE, D), FF_E ** -0.5, 0.1875, ((0, 32),))
    expert_ids_keys = jax.random.split(jax.random.fold_in(part_keys[9], 1), ROWS // ROWS_DEV)
    expert_ids_turns = jax.random.permutation(jax.random.fold_in(part_keys[9], 3), ROWS // ROWS_DEV)
    expert_ids = jax.vmap(lambda own, number: assign_block(jax.random.fold_in(part_keys[9], 2), own, number, ROWS_DEV, EXPERTS, TOP, CAPACITY, 2))(expert_ids_keys, expert_ids_turns).reshape((ROWS, TOP))
    gate_weights = jnp.clip(jnp.exp(math.log(1.0) - 2.3025851 * jax.random.uniform(part_keys[10], (ROWS, TOP), jnp.float32) ** level_of(part_keys[10], (ROWS, TOP), ((0, 32),), -0.2, 0.2)), 0.1, 1.0)
    placement = jax.random.permutation(key_of[11], N_TP).astype(jnp.int32)
    request_counts = uneven_parts(part_keys[12], N_TP, TOTAL_REQ, REQ_DEV, 2).astype(jnp.int32)
    return {"hidden_in": hidden_in, "norm_dense": norm_dense, "dense_gate": dense_gate, "dense_up": dense_up, "dense_down": dense_down, "norm_moe": norm_moe, "expert_gate": expert_gate, "expert_up": expert_up, "expert_down": expert_down, "expert_ids": expert_ids, "gate_weights": gate_weights, "placement": placement, "request_counts": request_counts}


epsilon = 1e-06

def rms_scale(values, scale_gain):
    widened = values.astype(jnp.float32)
    return widened * lax.rsqrt(lax.optimization_barrier(jnp.mean(widened * widened, axis=-1, keepdims=True)) + epsilon) * scale_gain

def reference(hidden_in, norm_dense, dense_gate, dense_up, dense_down, norm_moe, expert_gate, expert_up, expert_down, expert_ids, gate_weights, placement, request_counts):
    normed = rms_scale(hidden_in, norm_dense).astype(jnp.bfloat16)
    gate_proj = jnp.dot(normed, dense_gate, preferred_element_type=jnp.float32)
    up_proj = jnp.dot(normed, dense_up, preferred_element_type=jnp.float32)
    inner_act = (jax.nn.silu(gate_proj) * up_proj).astype(jnp.bfloat16)
    dense_sum = jnp.dot(inner_act, dense_down, preferred_element_type=jnp.float32)
    mixed_rows = (hidden_in.astype(jnp.float32) + dense_sum).astype(jnp.bfloat16)
    routed = rms_scale(mixed_rows, norm_moe).astype(jnp.bfloat16)

    def slice_term(running, slot_index):
        device = placement[slot_index]
        slice_gate = jnp.dot(routed, expert_gate[device], preferred_element_type=jnp.float32)
        slice_up = jnp.dot(routed, expert_up[device], preferred_element_type=jnp.float32)
        slice_hidden = (jax.nn.silu(slice_gate) * slice_up).astype(jnp.bfloat16)
        slice_out = lax.optimization_barrier(jnp.dot(slice_hidden, expert_down[device], preferred_element_type=jnp.float32).astype(jnp.bfloat16))
        row_weight = lax.optimization_barrier(jnp.sum(jnp.where(expert_ids == slot_index // SPLIT, gate_weights, 0.0), axis=1))
        return (running + row_weight[:, None] * slice_out.astype(jnp.float32), None)
    routed_sum, _ = lax.scan(slice_term, jnp.zeros((ROWS, D), jnp.float32), jnp.arange(N_TP, dtype=jnp.int32))
    result = (mixed_rows.astype(jnp.float32) + routed_sum).astype(jnp.bfloat16)
    slot_pos = jnp.arange(ROWS, dtype=jnp.int32)
    owner = slot_pos // ROWS_DEV
    live_rows = slot_pos % ROWS_DEV < DRAFT * request_counts[owner]
    layer_out = jnp.where(live_rows[:, None], result, jnp.zeros_like(result))
    return layer_out
```

```python
import functools

import jax
import jax.numpy as jnp
from jax import lax
from jax.experimental import pallas as pl
from jax.experimental.pallas import tpu as pltpu
from jax.sharding import PartitionSpec as P

SPLIT = 4
TOP = 4
DRAFT = 3
PAD = 8
HALF = 64
LANES = 128

epsilon = 1e-06


def rms_scale(widened, scale_gain):
    return (
        widened
        * lax.rsqrt(jnp.mean(widened * widened, axis=-1, keepdims=True) + epsilon)
        * scale_gain
    )


def kernel(
    n,
    hid,
    gain1,
    wg_hbm,
    wu_hbm,
    wd_hbm,
    gain2,
    eg_hbm,
    eu_hbm,
    ed_hbm,
    ids,
    gws,
    place,
    counts,
    out,
    wg,
    wu,
    wd,
    eg,
    eu,
    ed,
    pad_ref,
    mixed_ref,
    buf1,
    buf2,
    x2d,
    acc_g,
    acc_u,
    inner,
    acc_eg,
    acc_eu,
    inner_e,
    part,
    sbuf1,
    sbuf2,
    rbuf1,
    rbuf2,
    wsem,
    ssem,
    rsem,
):
    Z = n // 8
    rows = hid.shape[0]
    D = hid.shape[1]
    me = lax.axis_index("tp")
    c = lax.rem(me, 2)
    x = lax.rem(lax.div(me, 2), 2)
    y = lax.rem(lax.div(me, 4), 2)
    z = lax.div(me, 8)
    c_dev = me + 1 - 2 * c
    x_dev = me + 2 - 4 * x
    y_dev = me + 4 - 8 * y
    z_devs = [None] + [me + 8 * (lax.rem(z + j, Z) - z) for j in range(1, Z)]
    partners = [c_dev, x_dev, y_dev] + z_devs[1:]

    loads = [
        pltpu.make_async_copy(src, dst, wsem.at[i])
        for i, (src, dst) in enumerate(
            [
                (wg_hbm, wg),
                (wu_hbm, wu),
                (wd_hbm, wd),
                (eg_hbm.at[0], eg),
                (eu_hbm.at[0], eu),
                (ed_hbm.at[0], ed),
            ]
        )
    ]

    barrier = pltpu.get_barrier_semaphore()
    for dev in partners:
        pl.semaphore_signal(
            barrier, inc=1, device_id={"tp": dev}, device_id_type=pl.DeviceIdType.MESH
        )
    for load in loads:
        load.start()

    hidden = hid[...].astype(jnp.float32)
    pad_ref[...] = jnp.zeros_like(pad_ref)
    pad_ref[0:rows, :] = rms_scale(hidden, gain1[...])
    buf1[0] = pad_ref[...].astype(jnp.bfloat16)
    pl.semaphore_wait(barrier, len(partners))

    def remote(phase, src, dst, k, dev):
        return pltpu.make_async_remote_copy(
            src_ref=src,
            dst_ref=dst,
            send_sem=ssem.at[phase, k],
            recv_sem=rsem.at[phase, k],
            device_id={"tp": dev},
            device_id_type=pl.DeviceIdType.MESH,
        )

    def gather(phase, buf):
        def send(k, slot, dev):
            remote(phase, buf.at[k], buf.at[slot], slot, dev).start()

        def arrived(k):
            remote(phase, buf.at[k], buf.at[k], k, c_dev).wait_recv()

        send(0, 2 * Z, x_dev)
        send(0, Z, y_dev)
        for j in range(1, Z):
            send(0, j, z_devs[j])
        send(0, 4 * Z, c_dev)

        @pl.loop(1, Z)
        def _(k):
            arrived(k)
            send(k, 2 * Z + k, x_dev)
            send(k, Z + k, y_dev)
            send(k, 4 * Z + k, c_dev)

        @pl.loop(Z, 2 * Z)
        def _(k):
            arrived(k)
            send(k, 2 * Z + k, x_dev)
            send(k, 4 * Z + k, c_dev)

        @pl.loop(2 * Z, 4 * Z)
        def _(k):
            arrived(k)
            send(k, 4 * Z + k, c_dev)

        @pl.loop(4 * Z, 8 * Z)
        def _(k):
            arrived(k)

    def scatter(phase, sbuf, rbuf):
        def send(k, dev):
            remote(phase, sbuf.at[k], rbuf.at[k], k, dev).start()

        def arrived(k):
            remote(phase, sbuf.at[k], rbuf.at[k], k, c_dev).wait_recv()
            return rbuf[k].astype(jnp.float32)

        def first(k):
            sbuf[k] = part[k].astype(jnp.bfloat16)
            send(k, c_dev)

        pl.loop(6 * Z, 8 * Z)(first)
        pl.loop(5 * Z, 6 * Z)(first)
        pl.loop(4 * Z, 5 * Z)(first)

        @pl.loop(2 * Z, 4 * Z)
        def _(k):
            total = part[k] + arrived(4 * Z + k)
            sbuf[k] = total.astype(jnp.bfloat16)
            send(k, x_dev)

        @pl.loop(Z, 2 * Z)
        def _(k):
            total = part[k] + arrived(4 * Z + k) + arrived(2 * Z + k)
            sbuf[k] = total.astype(jnp.bfloat16)
            send(k, y_dev)

        for k in range(1, Z):
            total = part[k] + arrived(4 * Z + k) + arrived(2 * Z + k) + arrived(Z + k)
            sbuf[k] = total.astype(jnp.bfloat16)
            send(k, z_devs[Z - k])
        total = part[0] + arrived(4 * Z) + arrived(2 * Z) + arrived(Z)
        for k in range(1, Z):
            total = total + arrived(k)
        return total

    def flatten(buf):
        @pl.loop(0, n // 4)
        def _(b):
            block = buf[pl.ds(b * 4, 4), :, 0:D].astype(jnp.float32)
            x2d[pl.ds(pl.multiple_of(b * 4 * PAD, 4 * PAD), 4 * PAD), :] = block.reshape(
                4 * PAD, D
            ).astype(jnp.bfloat16)

    def project(gate_w, up_w, gate_acc, up_acc, result):
        step = 512
        gate_acc[...] = jnp.zeros_like(gate_acc)
        up_acc[...] = jnp.zeros_like(up_acc)

        @pl.loop(0, D // step)
        def _(i):
            span = pl.ds(pl.multiple_of(i * step, step), step)
            left = x2d[:, span]
            gate_acc[...] += jnp.dot(left, gate_w[span, :], preferred_element_type=jnp.float32)
            up_acc[...] += jnp.dot(left, up_w[span, :], preferred_element_type=jnp.float32)

        gate = gate_acc[...]
        result[...] = (gate / (1.0 + jnp.exp(-gate)) * up_acc[...]).astype(jnp.bfloat16)

    def down(act, down_w, scale):
        step = 512

        @pl.loop(0, D // step)
        def _(i):
            span = pl.ds(pl.multiple_of(i * step, step), step)
            value = jnp.dot(act[...], down_w[:, span], preferred_element_type=jnp.float32)
            value = value.reshape(n, PAD, step)
            part[:, :, span] = value if scale is None else value * scale

    gather(0, buf1)
    flatten(buf1)
    loads[0].wait()
    loads[1].wait()
    project(wg, wu, acc_g, acc_u, inner)
    loads[2].wait()
    down(inner, wd, None)
    dense_sum = scatter(1, sbuf1, rbuf1)

    mixed = (hid[...].astype(jnp.float32) + dense_sum[0:rows]).astype(jnp.bfloat16)
    mixed = mixed.astype(jnp.float32)
    mixed_ref[...] = mixed
    pad_ref[0:rows, :] = rms_scale(mixed, gain2[...])
    buf2[0, :, 0:D] = pad_ref[...].astype(jnp.bfloat16)
    lane = lax.broadcasted_iota(jnp.int32, (rows, LANES), 1)
    expert = lax.rem(lane, HALF)
    weight = jnp.zeros((rows, LANES), jnp.float32)
    for k in range(TOP):
        weight = weight + jnp.where(ids[:, k : k + 1] == expert, gws[:, k : k + 1], 0.0)
    high = weight.astype(jnp.bfloat16).astype(jnp.float32)
    pad_ref[0:rows, 0:LANES] = jnp.where(lane < HALF, high, weight - high)
    buf2[0, :, D : D + LANES] = pad_ref[:, 0:LANES].astype(jnp.bfloat16)

    gather(2, buf2)
    flatten(buf2)
    loads[3].wait()
    loads[4].wait()
    project(eg, eu, acc_eg, acc_eu, inner_e)
    slot = lax.broadcasted_iota(jnp.int32, (1, n), 1)
    hosted = jnp.sum(
        jnp.where(place[...] == me, lax.div(slot, SPLIT), 0).astype(jnp.float32),
        axis=1,
        keepdims=True,
    )
    lane3 = lax.rem(lax.broadcasted_iota(jnp.int32, (1, LANES), 1), HALF)
    chosen = jnp.where(lane3.astype(jnp.float32) == hosted, 1.0, 0.0)
    row_weight = jnp.sum(
        buf2[:, :, D : D + LANES].astype(jnp.float32) * chosen[None], axis=2, keepdims=True
    )
    loads[5].wait()
    down(inner_e, ed, row_weight)
    routed_sum = scatter(3, sbuf2, rbuf2)

    count = jnp.sum(
        jnp.where(slot == me, counts[...], 0).astype(jnp.float32), axis=1, keepdims=True
    )
    row = lax.broadcasted_iota(jnp.int32, (rows, 1), 0).astype(jnp.float32)
    final = mixed_ref[...] + routed_sum[0:rows]
    out[...] = jnp.where(row < DRAFT * count, final, 0.0).astype(out.dtype)

    @pl.loop(1, n)
    def _(k):
        remote(0, buf1.at[k], buf1.at[k], k, c_dev).wait_send()
        remote(1, sbuf1.at[k], rbuf1.at[k], k, c_dev).wait_send()
        remote(2, buf2.at[k], buf2.at[k], k, c_dev).wait_send()
        remote(3, sbuf2.at[k], rbuf2.at[k], k, c_dev).wait_send()


def body(
    hidden_in,
    norm_dense,
    dense_gate,
    dense_up,
    dense_down,
    norm_moe,
    expert_gate,
    expert_up,
    expert_down,
    expert_ids,
    gate_weights,
    placement,
    request_counts,
):
    n = lax.axis_size("tp")
    D = hidden_in.shape[1]
    F = dense_gate.shape[1]
    E = expert_gate.shape[2]
    vmem = pl.BlockSpec(memory_space=pltpu.VMEM)
    hbm = pl.BlockSpec(memory_space=pl.ANY)
    bf16, f32 = jnp.bfloat16, jnp.float32
    total_rows = n * PAD
    return pl.pallas_call(
        functools.partial(kernel, n),
        out_shape=jax.ShapeDtypeStruct(hidden_in.shape, hidden_in.dtype),
        in_specs=[vmem, vmem, hbm, hbm, hbm, vmem, hbm, hbm, hbm, vmem, vmem, vmem, vmem],
        out_specs=vmem,
        scratch_shapes=[
            pltpu.VMEM((D, F), bf16),
            pltpu.VMEM((D, F), bf16),
            pltpu.VMEM((F, D), bf16),
            pltpu.VMEM((D, E), bf16),
            pltpu.VMEM((D, E), bf16),
            pltpu.VMEM((E, D), bf16),
            pltpu.VMEM((PAD, D), f32),
            pltpu.VMEM(hidden_in.shape, f32),
            pltpu.VMEM((n, PAD, D), bf16),
            pltpu.VMEM((n, PAD, D + LANES), bf16),
            pltpu.VMEM((total_rows, D), bf16),
            pltpu.VMEM((total_rows, F), f32),
            pltpu.VMEM((total_rows, F), f32),
            pltpu.VMEM((total_rows, F), bf16),
            pltpu.VMEM((total_rows, E), f32),
            pltpu.VMEM((total_rows, E), f32),
            pltpu.VMEM((total_rows, E), bf16),
            pltpu.VMEM((n, PAD, D), f32),
            pltpu.VMEM((n, PAD, D), bf16),
            pltpu.VMEM((n, PAD, D), bf16),
            pltpu.VMEM((n, PAD, D), bf16),
            pltpu.VMEM((n, PAD, D), bf16),
            pltpu.SemaphoreType.DMA((6,)),
            pltpu.SemaphoreType.DMA((4, n)),
            pltpu.SemaphoreType.DMA((4, n)),
        ],
        compiler_params=pltpu.CompilerParams(
            collective_id=0, has_side_effects=True, vmem_limit_bytes=60 * 1024 * 1024
        ),
    )(
        hidden_in,
        norm_dense.reshape(1, D),
        dense_gate,
        dense_up,
        dense_down,
        norm_moe.reshape(1, D),
        expert_gate,
        expert_up,
        expert_down,
        expert_ids,
        gate_weights,
        placement.reshape(1, n),
        request_counts.reshape(1, n),
    )


def solution(mesh):
    in_specs = (
        P(("groups", "tp"), None),
        P(),
        P(None, "tp"),
        P(None, "tp"),
        P("tp", None),
        P(),
        P("tp", None, None),
        P("tp", None, None),
        P("tp", None, None),
        P(("groups", "tp"), None),
        P(("groups", "tp"), None),
        P(),
        P("groups"),
    )
    out_specs = P(("groups", "tp"), None)
    return jax.shard_map(body, mesh=mesh, in_specs=in_specs, out_specs=out_specs, check_vma=False)
```

```python
import functools

import jax
import jax.numpy as jnp
from jax import lax
from jax.experimental import pallas as pl
from jax.experimental.pallas import tpu as pltpu
from jax.sharding import PartitionSpec as P

SPLIT = 4
TOP = 4
DRAFT = 3
PAD = 8
HALF = 64
LANES = 128

epsilon = 1e-06


def rms_scale(widened, scale_gain):
    return (
        widened
        * lax.rsqrt(jnp.mean(widened * widened, axis=-1, keepdims=True) + epsilon)
        * scale_gain
    )


def kernel(
    n,
    hid,
    gain1,
    wg_hbm,
    wu_hbm,
    wd_hbm,
    gain2,
    eg_hbm,
    eu_hbm,
    ed_hbm,
    ids,
    gws,
    place,
    counts,
    out,
    wg,
    wu,
    wd,
    eg,
    eu,
    ed,
    pad_ref,
    mixed_ref,
    buf1,
    buf2,
    x2d,
    acc_g,
    acc_u,
    inner,
    acc_eg,
    acc_eu,
    inner_e,
    part,
    sbuf1,
    sbuf2,
    rbuf1,
    rbuf2,
    wsem,
    ssem,
    rsem,
):
    Z = n // 8
    rows = hid.shape[0]
    D = hid.shape[1]
    me = lax.axis_index("tp")
    c = lax.rem(me, 2)
    x = lax.rem(lax.div(me, 2), 2)
    y = lax.rem(lax.div(me, 4), 2)
    z = lax.div(me, 8)
    c_dev = me + 1 - 2 * c
    x_dev = me + 2 - 4 * x
    y_dev = me + 4 - 8 * y
    z_devs = [None] + [me + 8 * (lax.rem(z + j, Z) - z) for j in range(1, Z)]
    partners = [c_dev, x_dev, y_dev] + z_devs[1:]

    loads = [
        pltpu.make_async_copy(src, dst, wsem.at[i])
        for i, (src, dst) in enumerate(
            [
                (wg_hbm, wg),
                (wu_hbm, wu),
                (wd_hbm, wd),
                (eg_hbm.at[0], eg),
                (eu_hbm.at[0], eu),
                (ed_hbm.at[0], ed),
            ]
        )
    ]

    barrier = pltpu.get_barrier_semaphore()
    for dev in partners:
        pl.semaphore_signal(
            barrier, inc=1, device_id={"tp": dev}, device_id_type=pl.DeviceIdType.MESH
        )
    for load in loads:
        load.start()

    hidden = hid[...].astype(jnp.float32)
    pad_ref[...] = jnp.zeros_like(pad_ref)
    pad_ref[0:rows, :] = rms_scale(hidden, gain1[...].reshape(1, D))
    buf1[0] = pad_ref[...].astype(jnp.bfloat16)
    pl.semaphore_wait(barrier, len(partners))

    def remote(phase, src, dst, k, dev):
        return pltpu.make_async_remote_copy(
            src_ref=src,
            dst_ref=dst,
            send_sem=ssem.at[phase, k],
            recv_sem=rsem.at[phase, k],
            device_id={"tp": dev},
            device_id_type=pl.DeviceIdType.MESH,
        )

    def gather(phase, buf):
        def send(k, slot, dev):
            remote(phase, buf.at[k], buf.at[slot], slot, dev).start()

        def arrived(k):
            remote(phase, buf.at[k], buf.at[k], k, c_dev).wait_recv()

        send(0, 2 * Z, x_dev)
        send(0, Z, y_dev)
        for j in range(1, Z):
            send(0, j, z_devs[j])
        send(0, 4 * Z, c_dev)

        @pl.loop(1, Z)
        def _(k):
            arrived(k)
            send(k, 2 * Z + k, x_dev)
            send(k, Z + k, y_dev)
            send(k, 4 * Z + k, c_dev)

        @pl.loop(Z, 2 * Z)
        def _(k):
            arrived(k)
            send(k, 2 * Z + k, x_dev)
            send(k, 4 * Z + k, c_dev)

        @pl.loop(2 * Z, 4 * Z)
        def _(k):
            arrived(k)
            send(k, 4 * Z + k, c_dev)

        @pl.loop(4 * Z, 8 * Z)
        def _(k):
            arrived(k)

    def scatter(phase, sbuf, rbuf):
        def send(k, dev):
            remote(phase, sbuf.at[k], rbuf.at[k], k, dev).start()

        def arrived(k):
            remote(phase, sbuf.at[k], rbuf.at[k], k, c_dev).wait_recv()
            return rbuf[k].astype(jnp.float32)

        def first(k):
            sbuf[k] = part[k].astype(jnp.bfloat16)
            send(k, c_dev)

        pl.loop(6 * Z, 8 * Z)(first)
        pl.loop(5 * Z, 6 * Z)(first)
        pl.loop(4 * Z, 5 * Z)(first)

        @pl.loop(2 * Z, 4 * Z)
        def _(k):
            total = part[k] + arrived(4 * Z + k)
            sbuf[k] = total.astype(jnp.bfloat16)
            send(k, x_dev)

        @pl.loop(Z, 2 * Z)
        def _(k):
            total = part[k] + arrived(4 * Z + k) + arrived(2 * Z + k)
            sbuf[k] = total.astype(jnp.bfloat16)
            send(k, y_dev)

        for k in range(1, Z):
            total = part[k] + arrived(4 * Z + k) + arrived(2 * Z + k) + arrived(Z + k)
            sbuf[k] = total.astype(jnp.bfloat16)
            send(k, z_devs[Z - k])
        total = part[0] + arrived(4 * Z) + arrived(2 * Z) + arrived(Z)
        for k in range(1, Z):
            total = total + arrived(k)
        return total

    def flatten(buf):
        @pl.loop(0, n // 4)
        def _(b):
            block = buf[pl.ds(b * 4, 4), :, 0:D].astype(jnp.float32)
            x2d[pl.ds(pl.multiple_of(b * 4 * PAD, 4 * PAD), 4 * PAD), :] = block.reshape(
                4 * PAD, D
            ).astype(jnp.bfloat16)

    def project(gate_w, up_w, gate_acc, up_acc, result, columns):
        step = 512
        gate_acc[...] = jnp.zeros_like(gate_acc)
        up_acc[...] = jnp.zeros_like(up_acc)

        @pl.loop(0, D // step)
        def _(i):
            span = pl.ds(pl.multiple_of(i * step, step), step)
            left = x2d[:, span]
            for weight, total in ((gate_w, gate_acc), (up_w, up_acc)):
                tile = weight[:, span] if columns else weight[span, :]
                total[...] += lax.dot_general(
                    left,
                    tile,
                    (((1,), (1 if columns else 0,)), ((), ())),
                    preferred_element_type=jnp.float32,
                )

        gate = gate_acc[...]
        result[...] = (gate / (1.0 + jnp.exp(-gate)) * up_acc[...]).astype(jnp.bfloat16)

    def down(act, down_w, scale):
        step = 512

        @pl.loop(0, D // step)
        def _(i):
            span = pl.ds(pl.multiple_of(i * step, step), step)
            value = jnp.dot(act[...], down_w[:, span], preferred_element_type=jnp.float32)
            value = value.reshape(n, PAD, step)
            part[:, :, span] = value if scale is None else value * scale

    gather(0, buf1)
    flatten(buf1)
    loads[0].wait()
    loads[1].wait()
    project(wg, wu, acc_g, acc_u, inner, True)
    loads[2].wait()
    down(inner, wd, None)
    dense_sum = scatter(1, sbuf1, rbuf1)

    mixed = (hid[...].astype(jnp.float32) + dense_sum[0:rows]).astype(jnp.bfloat16)
    mixed = mixed.astype(jnp.float32)
    mixed_ref[...] = mixed
    pad_ref[0:rows, :] = rms_scale(mixed, gain2[...].reshape(1, D))
    buf2[0, :, 0:D] = pad_ref[...].astype(jnp.bfloat16)
    lane = lax.broadcasted_iota(jnp.int32, (1, LANES), 1)
    expert = lax.rem(lane, HALF)
    for r in range(rows):
        named = jnp.where(ids[:, r : r + 1] == expert, gws[:, r : r + 1], 0.0)
        weight = jnp.sum(named, axis=0, keepdims=True)
        high = weight.astype(jnp.bfloat16).astype(jnp.float32)
        pad_ref[r : r + 1, 0:LANES] = jnp.where(lane < HALF, high, weight - high)
    buf2[0, :, D : D + LANES] = pad_ref[:, 0:LANES].astype(jnp.bfloat16)

    gather(2, buf2)
    flatten(buf2)
    loads[3].wait()
    loads[4].wait()
    project(eg, eu, acc_eg, acc_eu, inner_e, False)
    slot = lax.broadcasted_iota(jnp.int32, (1, n), 1)
    hosted = jnp.sum(
        jnp.where(place[...] == me, lax.div(slot, SPLIT), 0).astype(jnp.float32),
        axis=1,
        keepdims=True,
    )
    chosen = jnp.where(expert.astype(jnp.float32) == hosted, 1.0, 0.0)
    row_weight = jnp.sum(
        buf2[:, :, D : D + LANES].astype(jnp.float32) * chosen[None], axis=2, keepdims=True
    )
    loads[5].wait()
    down(inner_e, ed, row_weight)
    routed_sum = scatter(3, sbuf2, rbuf2)

    count = jnp.sum(
        jnp.where(slot == me, counts[...], 0).astype(jnp.float32), axis=1, keepdims=True
    )
    row = lax.broadcasted_iota(jnp.int32, (rows, 1), 0).astype(jnp.float32)
    final = mixed_ref[...] + routed_sum[0:rows]
    out[...] = jnp.where(row < DRAFT * count, final, 0.0).astype(out.dtype)

    @pl.loop(1, n)
    def _(k):
        remote(0, buf1.at[k], buf1.at[k], k, c_dev).wait_send()
        remote(1, sbuf1.at[k], rbuf1.at[k], k, c_dev).wait_send()
        remote(2, buf2.at[k], buf2.at[k], k, c_dev).wait_send()
        remote(3, sbuf2.at[k], rbuf2.at[k], k, c_dev).wait_send()


def body(
    hidden_in,
    norm_dense,
    dense_gate,
    dense_up,
    dense_down,
    norm_moe,
    expert_gate,
    expert_up,
    expert_down,
    expert_ids,
    gate_weights,
    placement,
    request_counts,
):
    n = lax.axis_size("tp")
    D = hidden_in.shape[1]
    F = dense_gate.shape[1]
    E = expert_gate.shape[2]
    vmem = pl.BlockSpec(memory_space=pltpu.VMEM)
    hbm = pl.BlockSpec(memory_space=pl.ANY)
    bf16, f32 = jnp.bfloat16, jnp.float32
    total_rows = n * PAD
    return pl.pallas_call(
        functools.partial(kernel, n),
        out_shape=jax.ShapeDtypeStruct(hidden_in.shape, hidden_in.dtype),
        in_specs=[vmem, vmem, hbm, hbm, hbm, vmem, hbm, hbm, hbm, vmem, vmem, vmem, vmem],
        out_specs=vmem,
        scratch_shapes=[
            pltpu.VMEM((F, D), bf16),
            pltpu.VMEM((F, D), bf16),
            pltpu.VMEM((F, D), bf16),
            pltpu.VMEM((D, E), bf16),
            pltpu.VMEM((D, E), bf16),
            pltpu.VMEM((E, D), bf16),
            pltpu.VMEM((PAD, D), f32),
            pltpu.VMEM(hidden_in.shape, f32),
            pltpu.VMEM((n, PAD, D), bf16),
            pltpu.VMEM((n, PAD, D + LANES), bf16),
            pltpu.VMEM((total_rows, D), bf16),
            pltpu.VMEM((total_rows, F), f32),
            pltpu.VMEM((total_rows, F), f32),
            pltpu.VMEM((total_rows, F), bf16),
            pltpu.VMEM((total_rows, E), f32),
            pltpu.VMEM((total_rows, E), f32),
            pltpu.VMEM((total_rows, E), bf16),
            pltpu.VMEM((n, PAD, D), f32),
            pltpu.VMEM((n, PAD, D), bf16),
            pltpu.VMEM((n, PAD, D), bf16),
            pltpu.VMEM((n, PAD, D), bf16),
            pltpu.VMEM((n, PAD, D), bf16),
            pltpu.SemaphoreType.DMA((6,)),
            pltpu.SemaphoreType.DMA((4, n)),
            pltpu.SemaphoreType.DMA((4, n)),
        ],
        compiler_params=pltpu.CompilerParams(
            collective_id=0, has_side_effects=True, vmem_limit_bytes=60 * 1024 * 1024
        ),
    )(
        hidden_in,
        norm_dense,
        dense_gate.T,
        dense_up.T,
        dense_down,
        norm_moe,
        expert_gate,
        expert_up,
        expert_down,
        expert_ids.T,
        gate_weights.T,
        placement.reshape(1, n),
        request_counts.reshape(1, n),
    )


def solution(mesh):
    in_specs = (
        P(("groups", "tp"), None),
        P(),
        P(None, "tp"),
        P(None, "tp"),
        P("tp", None),
        P(),
        P("tp", None, None),
        P("tp", None, None),
        P("tp", None, None),
        P(("groups", "tp"), None),
        P(("groups", "tp"), None),
        P(),
        P("groups"),
    )
    out_specs = P(("groups", "tp"), None)
    return jax.shard_map(body, mesh=mesh, in_specs=in_specs, out_specs=out_specs, check_vma=False)
```

```python
import functools

import jax
import jax.numpy as jnp
from jax import lax
from jax.experimental import pallas as pl
from jax.experimental.pallas import tpu as pltpu
from jax.sharding import PartitionSpec as P

SPLIT = 4
TOP = 4
DRAFT = 3
PAD = 8
HALF = 64
LANES = 128

epsilon = 1e-06


def rms_scale(widened, scale_gain):
    return (
        widened
        * lax.rsqrt(jnp.mean(widened * widened, axis=-1, keepdims=True) + epsilon)
        * scale_gain
    )


def kernel(
    n,
    hid,
    gain1,
    wg_hbm,
    wu_hbm,
    wd_hbm,
    gain2,
    eg_hbm,
    eu_hbm,
    ed_hbm,
    ids,
    gws,
    place,
    counts,
    out,
    wg,
    wu,
    wd,
    eg,
    eu,
    ed,
    pad_ref,
    mixed_ref,
    sum_ref,
    buf1a,
    buf1b,
    buf2a,
    buf2b,
    x2d,
    acc_g,
    acc_u,
    inner,
    acc_eg,
    acc_eu,
    inner_e,
    part,
    sbuf1a,
    sbuf1b,
    sbuf2a,
    sbuf2b,
    rbuf1a,
    rbuf1b,
    rbuf2a,
    rbuf2b,
    wsem,
    ssem,
    rsem,
):
    Z = n // 8
    rows = hid.shape[0]
    D = hid.shape[1]
    W = D // 2
    me = lax.axis_index("tp")
    c = lax.rem(me, 2)
    x = lax.rem(lax.div(me, 2), 2)
    y = lax.rem(lax.div(me, 4), 2)
    z = lax.div(me, 8)
    c_dev = me + 1 - 2 * c
    x_dev = me + 2 - 4 * x
    y_dev = me + 4 - 8 * y
    z_devs = [None] + [me + 8 * (lax.rem(z + j, Z) - z) for j in range(1, Z)]
    partners = [c_dev, x_dev, y_dev] + z_devs[1:]

    loads = [
        pltpu.make_async_copy(src, dst, wsem.at[i])
        for i, (src, dst) in enumerate(
            [
                (wg_hbm, wg),
                (wu_hbm, wu),
                (wd_hbm, wd),
                (eg_hbm.at[0], eg),
                (eu_hbm.at[0], eu),
                (ed_hbm.at[0], ed),
            ]
        )
    ]

    barrier = pltpu.get_barrier_semaphore()
    for dev in partners:
        pl.semaphore_signal(
            barrier, inc=1, device_id={"tp": dev}, device_id_type=pl.DeviceIdType.MESH
        )
    for load in loads:
        load.start()

    hidden = hid[...].astype(jnp.float32)
    pad_ref[...] = jnp.zeros_like(pad_ref)
    pad_ref[0:rows, :] = rms_scale(hidden, gain1[...].reshape(1, D))
    buf1a[0] = pad_ref[:, 0:W].astype(jnp.bfloat16)
    buf1b[0] = pad_ref[:, W:D].astype(jnp.bfloat16)
    pl.semaphore_wait(barrier, len(partners))

    def remote(phase, half, src, dst, k, dev):
        return pltpu.make_async_remote_copy(
            src_ref=src,
            dst_ref=dst,
            send_sem=ssem.at[phase, half],
            recv_sem=rsem.at[phase, half, k],
            device_id={"tp": dev},
            device_id_type=pl.DeviceIdType.MESH,
        )

    steps = ((y_dev, x_dev), (x_dev, y_dev))

    def place_of(half, group):
        return group if half == 0 else (0, 2, 1, 3, 4, 6, 5, 7)[group]

    def gather(phase, bufs):
        def send(half, k, slot, dev):
            buf = bufs[half]
            remote(phase, half, buf.at[k], buf.at[slot], slot, dev).start()

        def to_core(half, k):
            buf = bufs[half]
            remote(phase, half, buf.at[k], buf.at[4 * Z + k], 0, c_dev).start()

        def arrived(half, k):
            buf = bufs[half]
            remote(phase, half, buf.at[k], buf.at[k], k, c_dev).wait_recv()

        for half in range(2):
            send(half, 0, 2 * Z, steps[half][1])
            send(half, 0, Z, steps[half][0])
        for j in range(1, Z):
            for half in range(2):
                send(half, 0, j, z_devs[j])
        for half in range(2):
            to_core(half, 0)

        @pl.loop(1, Z)
        def _(k):
            for half in range(2):
                arrived(half, k)
                send(half, k, 2 * Z + k, steps[half][1])
                send(half, k, Z + k, steps[half][0])
                to_core(half, k)

        @pl.loop(Z, 2 * Z)
        def _(k):
            for half in range(2):
                arrived(half, k)
                send(half, k, 2 * Z + k, steps[half][1])
                to_core(half, k)

        @pl.loop(2 * Z, 4 * Z)
        def _(k):
            for half in range(2):
                arrived(half, k)
                to_core(half, k)

        for half in range(2):
            span = bufs[half].at[pl.ds(4 * Z, 4 * Z)]
            remote(phase, half, span, span, 0, c_dev).wait_recv()

    def open_scatter(phase, half, sbuf, rbuf):
        base = half * W
        for group in (7, 6, 5, 4):

            @pl.loop(0, Z)
            def _(i):
                k = group * Z + (Z - 1 - i)
                row = place_of(half, group) * Z + (Z - 1 - i)
                sbuf[k] = part[row, :, base : base + W].astype(jnp.bfloat16)
                remote(phase, half, sbuf.at[k], rbuf.at[k], k, c_dev).start()

    def scatter(phase, sbufs, rbufs):
        def send(half, k, dev):
            sbuf, rbuf = sbufs[half], rbufs[half]
            remote(phase, half, sbuf.at[k], rbuf.at[k], k, dev).start()

        def arrived(half, k):
            rbuf = rbufs[half]
            remote(phase, half, rbuf.at[k], rbuf.at[k], k, c_dev).wait_recv()
            return rbuf[k].astype(jnp.float32)

        def own(half, group, i):
            return part[place_of(half, group) * Z + i, :, half * W : half * W + W]

        for group in (3, 2):

            @pl.loop(0, Z)
            def _(i):
                j = Z - 1 - i
                k = group * Z + j
                for half in range(2):
                    total = own(half, group, j) + arrived(half, 4 * Z + k)
                    sbufs[half][k] = total.astype(jnp.bfloat16)
                    send(half, k, steps[half][1])

        @pl.loop(0, Z)
        def _(i):
            j = Z - 1 - i
            k = Z + j
            for half in range(2):
                total = own(half, 1, j) + arrived(half, 4 * Z + k) + arrived(half, 2 * Z + k)
                sbufs[half][k] = total.astype(jnp.bfloat16)
                send(half, k, steps[half][0])

        for k in reversed(range(1, Z)):
            for half in range(2):
                total = own(half, 0, k) + arrived(half, 4 * Z + k)
                total = total + arrived(half, 2 * Z + k) + arrived(half, Z + k)
                sbufs[half][k] = total.astype(jnp.bfloat16)
                send(half, k, z_devs[Z - k])
        for half in range(2):
            total = own(half, 0, 0)
            for k in (4 * Z, 2 * Z, Z) + tuple(reversed(range(1, Z))):
                total = total + arrived(half, k)
            sum_ref[:, half * W : half * W + W] = total

    def flatten(bufs):
        for half in range(2):
            for group in range(8):
                block = bufs[half][group * Z : group * Z + Z, :, 0:W].astype(jnp.float32)
                row = place_of(half, group) * Z * PAD
                x2d[row : row + Z * PAD, half * W : half * W + W] = block.reshape(
                    Z * PAD, W
                ).astype(jnp.bfloat16)

    def project(gate_w, up_w, gate_acc, up_acc, result, columns):
        step = 512
        gate_acc[...] = jnp.zeros_like(gate_acc)
        up_acc[...] = jnp.zeros_like(up_acc)

        @pl.loop(0, D // step)
        def _(i):
            span = pl.ds(pl.multiple_of(i * step, step), step)
            left = x2d[:, span]
            for weight, total in ((gate_w, gate_acc), (up_w, up_acc)):
                tile = weight[:, span] if columns else weight[span, :]
                total[...] += lax.dot_general(
                    left,
                    tile,
                    (((1,), (1 if columns else 0,)), ((), ())),
                    preferred_element_type=jnp.float32,
                )

        gate = gate_acc[...]
        result[...] = (gate / (1.0 + jnp.exp(-gate)) * up_acc[...]).astype(jnp.bfloat16)

    def down(act, down_w, scale, half):
        step = 256

        @pl.loop(0, W // step)
        def _(i):
            span = pl.ds(pl.multiple_of(half * W + i * step, step), step)
            value = jnp.dot(act[...], down_w[:, span], preferred_element_type=jnp.float32)
            value = value.reshape(n, PAD, step)
            part[:, :, span] = value if scale is None else value * scale

    buf1, buf2 = (buf1a, buf1b), (buf2a, buf2b)
    sbuf1, sbuf2 = (sbuf1a, sbuf1b), (sbuf2a, sbuf2b)
    rbuf1, rbuf2 = (rbuf1a, rbuf1b), (rbuf2a, rbuf2b)
    gather(0, buf1)
    flatten(buf1)
    loads[0].wait()
    loads[1].wait()
    project(wg, wu, acc_g, acc_u, inner, True)
    loads[2].wait()
    for half in range(2):
        down(inner, wd, None, half)
        open_scatter(1, half, sbuf1[half], rbuf1[half])
    scatter(1, sbuf1, rbuf1)

    mixed = (hid[...].astype(jnp.float32) + sum_ref[0:rows, :]).astype(jnp.bfloat16)
    mixed = mixed.astype(jnp.float32)
    mixed_ref[...] = mixed
    pad_ref[0:rows, :] = rms_scale(mixed, gain2[...].reshape(1, D))
    buf2a[0, :, 0:W] = pad_ref[:, 0:W].astype(jnp.bfloat16)
    buf2b[0] = pad_ref[:, W:D].astype(jnp.bfloat16)
    lane = lax.broadcasted_iota(jnp.int32, (1, LANES), 1)
    expert = lax.rem(lane, HALF)
    for r in range(rows):
        named = jnp.where(ids[:, r : r + 1] == expert, gws[:, r : r + 1], 0.0)
        weight = jnp.sum(named, axis=0, keepdims=True)
        high = weight.astype(jnp.bfloat16).astype(jnp.float32)
        pad_ref[r : r + 1, 0:LANES] = jnp.where(lane < HALF, high, weight - high)
    buf2a[0, :, W : W + LANES] = pad_ref[:, 0:LANES].astype(jnp.bfloat16)

    gather(2, buf2)
    flatten(buf2)
    loads[3].wait()
    loads[4].wait()
    project(eg, eu, acc_eg, acc_eu, inner_e, False)
    slot = lax.broadcasted_iota(jnp.int32, (1, n), 1)
    hosted = jnp.sum(
        jnp.where(place[...] == me, lax.div(slot, SPLIT), 0).astype(jnp.float32),
        axis=1,
        keepdims=True,
    )
    chosen = jnp.where(expert.astype(jnp.float32) == hosted, 1.0, 0.0)
    row_weight = jnp.sum(
        buf2a[:, :, W : W + LANES].astype(jnp.float32) * chosen[None], axis=2, keepdims=True
    )
    loads[5].wait()
    for half in range(2):
        down(inner_e, ed, row_weight, half)
        open_scatter(3, half, sbuf2[half], rbuf2[half])
    scatter(3, sbuf2, rbuf2)

    count = jnp.sum(
        jnp.where(slot == me, counts[...], 0).astype(jnp.float32), axis=1, keepdims=True
    )
    row = lax.broadcasted_iota(jnp.int32, (rows, 1), 0).astype(jnp.float32)
    final = mixed_ref[...] + sum_ref[0:rows, :]
    out[...] = jnp.where(row < DRAFT * count, final, 0.0).astype(out.dtype)

    for phase, sent in enumerate((buf1, sbuf1, buf2, sbuf2)):
        for half in range(2):
            span = sent[half].at[pl.ds(1, n - 1)]
            remote(phase, half, span, span, 0, c_dev).wait_send()


def body(
    hidden_in,
    norm_dense,
    dense_gate,
    dense_up,
    dense_down,
    norm_moe,
    expert_gate,
    expert_up,
    expert_down,
    expert_ids,
    gate_weights,
    placement,
    request_counts,
):
    n = lax.axis_size("tp")
    D = hidden_in.shape[1]
    F = dense_gate.shape[1]
    E = expert_gate.shape[2]
    vmem = pl.BlockSpec(memory_space=pltpu.VMEM)
    hbm = pl.BlockSpec(memory_space=pl.ANY)
    bf16, f32 = jnp.bfloat16, jnp.float32
    total_rows = n * PAD
    return pl.pallas_call(
        functools.partial(kernel, n),
        out_shape=jax.ShapeDtypeStruct(hidden_in.shape, hidden_in.dtype),
        in_specs=[vmem, vmem, hbm, hbm, hbm, vmem, hbm, hbm, hbm, vmem, vmem, vmem, vmem],
        out_specs=vmem,
        scratch_shapes=[
            pltpu.VMEM((F, D), bf16),
            pltpu.VMEM((F, D), bf16),
            pltpu.VMEM((F, D), bf16),
            pltpu.VMEM((D, E), bf16),
            pltpu.VMEM((D, E), bf16),
            pltpu.VMEM((E, D), bf16),
            pltpu.VMEM((PAD, D), f32),
            pltpu.VMEM(hidden_in.shape, f32),
            pltpu.VMEM((PAD, D), f32),
            pltpu.VMEM((n, PAD, D // 2), bf16),
            pltpu.VMEM((n, PAD, D // 2), bf16),
            pltpu.VMEM((n, PAD, D // 2 + LANES), bf16),
            pltpu.VMEM((n, PAD, D // 2), bf16),
            pltpu.VMEM((total_rows, D), bf16),
            pltpu.VMEM((total_rows, F), f32),
            pltpu.VMEM((total_rows, F), f32),
            pltpu.VMEM((total_rows, F), bf16),
            pltpu.VMEM((total_rows, E), f32),
            pltpu.VMEM((total_rows, E), f32),
            pltpu.VMEM((total_rows, E), bf16),
            pltpu.VMEM((n, PAD, D), f32),
            *[pltpu.VMEM((n, PAD, D // 2), bf16)] * 8,
            pltpu.SemaphoreType.DMA((6,)),
            pltpu.SemaphoreType.DMA((4, 2)),
            pltpu.SemaphoreType.DMA((4, 2, n)),
        ],
        compiler_params=pltpu.CompilerParams(
            collective_id=0, has_side_effects=True, vmem_limit_bytes=60 * 1024 * 1024
        ),
    )(
        hidden_in,
        norm_dense,
        dense_gate.T,
        dense_up.T,
        dense_down,
        norm_moe,
        expert_gate,
        expert_up,
        expert_down,
        expert_ids.T,
        gate_weights.T,
        placement.reshape(1, n),
        request_counts.reshape(1, n),
    )


def solution(mesh):
    in_specs = (
        P(("groups", "tp"), None),
        P(),
        P(None, "tp"),
        P(None, "tp"),
        P("tp", None),
        P(),
        P("tp", None, None),
        P("tp", None, None),
        P("tp", None, None),
        P(("groups", "tp"), None),
        P(("groups", "tp"), None),
        P(),
        P("groups"),
    )
    out_specs = P(("groups", "tp"), None)
    return jax.shard_map(body, mesh=mesh, in_specs=in_specs, out_specs=out_specs, check_vma=False)
```

```python
import functools

import jax
import jax.numpy as jnp
from jax import lax
from jax.experimental import pallas as pl
from jax.experimental.pallas import tpu as pltpu
from jax.sharding import PartitionSpec as P

SPLIT = 4
TOP = 4
DRAFT = 3
PAD = 8
HALF = 64
LANES = 128

epsilon = 1e-06


def rms_scale(widened, scale_gain):
    return (
        widened
        * lax.rsqrt(jnp.mean(widened * widened, axis=-1, keepdims=True) + epsilon)
        * scale_gain
    )


def kernel(
    n,
    hid,
    gain1,
    wg_hbm,
    wu_hbm,
    wd_hbm,
    gain2,
    eg_hbm,
    eu_hbm,
    ed_hbm,
    ids,
    gws,
    place,
    counts,
    out,
    wg,
    wu,
    wd,
    eg,
    eu,
    ed,
    pad_ref,
    mixed_ref,
    sum_ref,
    buf1a,
    buf1b,
    buf2a,
    buf2b,
    x2d,
    acc_g,
    acc_u,
    inner,
    acc_eg,
    acc_eu,
    inner_e,
    part,
    sbuf1a,
    sbuf1b,
    sbuf2a,
    sbuf2b,
    rbuf1a,
    rbuf1b,
    rbuf2a,
    rbuf2b,
    wsem,
    ssem,
    rsem,
):
    Z = n // 8
    rows = hid.shape[0]
    D = hid.shape[1]
    W = D // 2
    me = lax.axis_index("tp")
    c = lax.rem(me, 2)
    x = lax.rem(lax.div(me, 2), 2)
    y = lax.rem(lax.div(me, 4), 2)
    z = lax.div(me, 8)
    c_dev = me + 1 - 2 * c
    x_dev = me + 2 - 4 * x
    y_dev = me + 4 - 8 * y
    z_devs = [None] + [me + 8 * (lax.rem(z + j, Z) - z) for j in range(1, Z)]
    partners = [c_dev, x_dev, y_dev] + z_devs[1:]

    loads = [
        pltpu.make_async_copy(src, dst, wsem.at[i])
        for i, (src, dst) in enumerate(
            [
                (wg_hbm, wg),
                (wu_hbm, wu),
                (wd_hbm, wd),
                (eg_hbm.at[0], eg),
                (eu_hbm.at[0], eu),
                (ed_hbm.at[0], ed),
            ]
        )
    ]

    barrier = pltpu.get_barrier_semaphore()
    for dev in partners:
        pl.semaphore_signal(
            barrier, inc=1, device_id={"tp": dev}, device_id_type=pl.DeviceIdType.MESH
        )
    for load in loads:
        load.start()

    hidden = hid[...].astype(jnp.float32)
    pad_ref[...] = jnp.zeros_like(pad_ref)
    pad_ref[0:rows, :] = rms_scale(hidden, gain1[...].reshape(1, D))
    buf1a[0] = pad_ref[:, 0:W].astype(jnp.bfloat16)
    buf1b[0] = pad_ref[:, W:D].astype(jnp.bfloat16)
    pl.semaphore_wait(barrier, len(partners))

    def remote(phase, half, src, dst, k, dev):
        return pltpu.make_async_remote_copy(
            src_ref=src,
            dst_ref=dst,
            send_sem=ssem.at[phase, half],
            recv_sem=rsem.at[phase, half, k],
            device_id={"tp": dev},
            device_id_type=pl.DeviceIdType.MESH,
        )

    steps = ((y_dev, x_dev), (x_dev, y_dev))

    def place_of(half, group):
        return group if half == 0 else (0, 2, 1, 3, 4, 6, 5, 7)[group]

    def gather(phase, bufs):
        def send(half, k, slot, dev):
            buf = bufs[half]
            remote(phase, half, buf.at[k], buf.at[slot], slot, dev).start()

        def to_core(half, k):
            buf = bufs[half]
            remote(phase, half, buf.at[k], buf.at[4 * Z + k], 0, c_dev).start()

        def arrived(half, k):
            buf = bufs[half]
            remote(phase, half, buf.at[k], buf.at[k], k, c_dev).wait_recv()

        for half in range(2):
            send(half, 0, 2 * Z, steps[half][1])
            send(half, 0, Z, steps[half][0])
        for j in range(1, Z):
            for half in range(2):
                send(half, 0, j, z_devs[j])
        for half in range(2):
            to_core(half, 0)

        @pl.loop(1, Z)
        def _(k):
            for half in range(2):
                arrived(half, k)
                send(half, k, 2 * Z + k, steps[half][1])
                send(half, k, Z + k, steps[half][0])
                to_core(half, k)

        @pl.loop(Z, 2 * Z)
        def _(k):
            for half in range(2):
                arrived(half, k)
                send(half, k, 2 * Z + k, steps[half][1])
                to_core(half, k)

        @pl.loop(2 * Z, 4 * Z)
        def _(k):
            for half in range(2):
                arrived(half, k)
                to_core(half, k)

    def open_scatter(phase, half, sbuf, rbuf):
        base = half * W
        for group in (7, 6, 5, 4):

            @pl.loop(0, Z)
            def _(i):
                k = group * Z + (Z - 1 - i)
                row = place_of(half, group) * Z + (Z - 1 - i)
                sbuf[k] = part[row, :, base : base + W].astype(jnp.bfloat16)
                remote(phase, half, sbuf.at[k], rbuf.at[k], k, c_dev).start()

    def scatter(phase, sbufs, rbufs):
        def send(half, k, dev):
            sbuf, rbuf = sbufs[half], rbufs[half]
            remote(phase, half, sbuf.at[k], rbuf.at[k], k, dev).start()

        def arrived(half, k):
            rbuf = rbufs[half]
            remote(phase, half, rbuf.at[k], rbuf.at[k], k, c_dev).wait_recv()
            return rbuf[k].astype(jnp.float32)

        def own(half, group, i):
            return part[place_of(half, group) * Z + i, :, half * W : half * W + W]

        for group in (3, 2):

            @pl.loop(0, Z)
            def _(i):
                j = Z - 1 - i
                k = group * Z + j
                for half in range(2):
                    total = own(half, group, j) + arrived(half, 4 * Z + k)
                    sbufs[half][k] = total.astype(jnp.bfloat16)
                    send(half, k, steps[half][1])

        @pl.loop(0, Z)
        def _(i):
            j = Z - 1 - i
            k = Z + j
            for half in range(2):
                total = own(half, 1, j) + arrived(half, 4 * Z + k) + arrived(half, 2 * Z + k)
                sbufs[half][k] = total.astype(jnp.bfloat16)
                send(half, k, steps[half][0])

        for k in reversed(range(1, Z)):
            for half in range(2):
                total = own(half, 0, k) + arrived(half, 4 * Z + k)
                total = total + arrived(half, 2 * Z + k) + arrived(half, Z + k)
                sbufs[half][k] = total.astype(jnp.bfloat16)
                send(half, k, z_devs[Z - k])
        for half in range(2):
            total = own(half, 0, 0)
            for k in (4 * Z, 2 * Z, Z) + tuple(reversed(range(1, Z))):
                total = total + arrived(half, k)
            sum_ref[:, half * W : half * W + W] = total

    def flatten(phase, bufs):
        for late in range(2):
            for half in range(2):
                if late:
                    span = bufs[half].at[pl.ds(4 * Z, 4 * Z)]
                    remote(phase, half, span, span, 0, c_dev).wait_recv()
                for group in range(4 * late, 4 * late + 4):
                    block = bufs[half][group * Z : group * Z + Z, :, 0:W].astype(jnp.float32)
                    row = place_of(half, group) * Z * PAD
                    x2d[row : row + Z * PAD, half * W : half * W + W] = block.reshape(
                        Z * PAD, W
                    ).astype(jnp.bfloat16)

    def project(gate_w, up_w, gate_acc, up_acc, result, columns):
        step = 512
        gate_acc[...] = jnp.zeros_like(gate_acc)
        up_acc[...] = jnp.zeros_like(up_acc)

        @pl.loop(0, D // step)
        def _(i):
            span = pl.ds(pl.multiple_of(i * step, step), step)
            left = x2d[:, span]
            for weight, total in ((gate_w, gate_acc), (up_w, up_acc)):
                tile = weight[:, span] if columns else weight[span, :]
                total[...] += lax.dot_general(
                    left,
                    tile,
                    (((1,), (1 if columns else 0,)), ((), ())),
                    preferred_element_type=jnp.float32,
                )

        gate = gate_acc[...]
        result[...] = (gate / (1.0 + jnp.exp(-gate)) * up_acc[...]).astype(jnp.bfloat16)

    def down(act, down_w, scale, half):
        step = 256

        @pl.loop(0, W // step)
        def _(i):
            span = pl.ds(pl.multiple_of(half * W + i * step, step), step)
            value = jnp.dot(act[...], down_w[:, span], preferred_element_type=jnp.float32)
            value = value.reshape(n, PAD, step)
            part[:, :, span] = value if scale is None else value * scale

    buf1, buf2 = (buf1a, buf1b), (buf2a, buf2b)
    sbuf1, sbuf2 = (sbuf1a, sbuf1b), (sbuf2a, sbuf2b)
    rbuf1, rbuf2 = (rbuf1a, rbuf1b), (rbuf2a, rbuf2b)
    gather(0, buf1)
    flatten(0, buf1)
    loads[0].wait()
    loads[1].wait()
    project(wg, wu, acc_g, acc_u, inner, True)
    loads[2].wait()
    for half in range(2):
        down(inner, wd, None, half)
        open_scatter(1, half, sbuf1[half], rbuf1[half])
    scatter(1, sbuf1, rbuf1)

    mixed = (hid[...].astype(jnp.float32) + sum_ref[0:rows, :]).astype(jnp.bfloat16)
    mixed = mixed.astype(jnp.float32)
    mixed_ref[...] = mixed
    pad_ref[0:rows, :] = rms_scale(mixed, gain2[...].reshape(1, D))
    buf2a[0, :, 0:W] = pad_ref[:, 0:W].astype(jnp.bfloat16)
    buf2b[0] = pad_ref[:, W:D].astype(jnp.bfloat16)
    lane = lax.broadcasted_iota(jnp.int32, (1, LANES), 1)
    expert = lax.rem(lane, HALF)
    for r in range(rows):
        named = jnp.where(ids[:, r : r + 1] == expert, gws[:, r : r + 1], 0.0)
        weight = jnp.sum(named, axis=0, keepdims=True)
        high = weight.astype(jnp.bfloat16).astype(jnp.float32)
        pad_ref[r : r + 1, 0:LANES] = jnp.where(lane < HALF, high, weight - high)
    buf2a[0, :, W : W + LANES] = pad_ref[:, 0:LANES].astype(jnp.bfloat16)

    gather(2, buf2)
    flatten(2, buf2)
    loads[3].wait()
    loads[4].wait()
    project(eg, eu, acc_eg, acc_eu, inner_e, False)
    slot = lax.broadcasted_iota(jnp.int32, (1, n), 1)
    hosted = jnp.sum(
        jnp.where(place[...] == me, lax.div(slot, SPLIT), 0).astype(jnp.float32),
        axis=1,
        keepdims=True,
    )
    chosen = jnp.where(expert.astype(jnp.float32) == hosted, 1.0, 0.0)
    row_weight = jnp.sum(
        buf2a[:, :, W : W + LANES].astype(jnp.float32) * chosen[None], axis=2, keepdims=True
    )
    loads[5].wait()
    for half in range(2):
        down(inner_e, ed, row_weight, half)
        open_scatter(3, half, sbuf2[half], rbuf2[half])
    scatter(3, sbuf2, rbuf2)

    count = jnp.sum(
        jnp.where(slot == me, counts[...], 0).astype(jnp.float32), axis=1, keepdims=True
    )
    row = lax.broadcasted_iota(jnp.int32, (rows, 1), 0).astype(jnp.float32)
    final = mixed_ref[...] + sum_ref[0:rows, :]
    out[...] = jnp.where(row < DRAFT * count, final, 0.0).astype(out.dtype)

    for phase, sent in enumerate((buf1, sbuf1, buf2, sbuf2)):
        for half in range(2):
            span = sent[half].at[pl.ds(1, n - 1)]
            remote(phase, half, span, span, 0, c_dev).wait_send()


def body(
    hidden_in,
    norm_dense,
    dense_gate,
    dense_up,
    dense_down,
    norm_moe,
    expert_gate,
    expert_up,
    expert_down,
    expert_ids,
    gate_weights,
    placement,
    request_counts,
):
    n = lax.axis_size("tp")
    D = hidden_in.shape[1]
    F = dense_gate.shape[1]
    E = expert_gate.shape[2]
    vmem = pl.BlockSpec(memory_space=pltpu.VMEM)
    hbm = pl.BlockSpec(memory_space=pl.ANY)
    bf16, f32 = jnp.bfloat16, jnp.float32
    total_rows = n * PAD
    return pl.pallas_call(
        functools.partial(kernel, n),
        out_shape=jax.ShapeDtypeStruct(hidden_in.shape, hidden_in.dtype),
        in_specs=[vmem, vmem, hbm, hbm, hbm, vmem, hbm, hbm, hbm, vmem, vmem, vmem, vmem],
        out_specs=vmem,
        scratch_shapes=[
            pltpu.VMEM((F, D), bf16),
            pltpu.VMEM((F, D), bf16),
            pltpu.VMEM((F, D), bf16),
            pltpu.VMEM((D, E), bf16),
            pltpu.VMEM((D, E), bf16),
            pltpu.VMEM((E, D), bf16),
            pltpu.VMEM((PAD, D), f32),
            pltpu.VMEM(hidden_in.shape, f32),
            pltpu.VMEM((PAD, D), f32),
            pltpu.VMEM((n, PAD, D // 2), bf16),
            pltpu.VMEM((n, PAD, D // 2), bf16),
            pltpu.VMEM((n, PAD, D // 2 + LANES), bf16),
            pltpu.VMEM((n, PAD, D // 2), bf16),
            pltpu.VMEM((total_rows, D), bf16),
            pltpu.VMEM((total_rows, F), f32),
            pltpu.VMEM((total_rows, F), f32),
            pltpu.VMEM((total_rows, F), bf16),
            pltpu.VMEM((total_rows, E), f32),
            pltpu.VMEM((total_rows, E), f32),
            pltpu.VMEM((total_rows, E), bf16),
            pltpu.VMEM((n, PAD, D), f32),
            *[pltpu.VMEM((n, PAD, D // 2), bf16)] * 8,
            pltpu.SemaphoreType.DMA((6,)),
            pltpu.SemaphoreType.DMA((4, 2)),
            pltpu.SemaphoreType.DMA((4, 2, n)),
        ],
        compiler_params=pltpu.CompilerParams(
            collective_id=0, has_side_effects=True, vmem_limit_bytes=60 * 1024 * 1024
        ),
    )(
        hidden_in,
        norm_dense,
        dense_gate.T,
        dense_up.T,
        dense_down,
        norm_moe,
        expert_gate,
        expert_up,
        expert_down,
        expert_ids.T,
        gate_weights.T,
        placement.reshape(1, n),
        request_counts.reshape(1, n),
    )


def solution(mesh):
    in_specs = (
        P(("groups", "tp"), None),
        P(),
        P(None, "tp"),
        P(None, "tp"),
        P("tp", None),
        P(),
        P("tp", None, None),
        P("tp", None, None),
        P("tp", None, None),
        P(("groups", "tp"), None),
        P(("groups", "tp"), None),
        P(),
        P("groups"),
    )
    out_specs = P(("groups", "tp"), None)
    return jax.shard_map(body, mesh=mesh, in_specs=in_specs, out_specs=out_specs, check_vma=False)
```
